32 devices in a mesh: lang: 4 (over x, core), fsdp: 2 (over y), dp: 4 (over z).
Axes of the slice: x: 2, y: 2, z: 4, core: 2. Of those that a mesh axis runs over, the one named last changes fastest.
Arguments:
- tokens_in: bfloat16 [1024, 8192], P('dp'), may hold values from -6 to 6
- cotangent: bfloat16 [1024, 16384], P('dp', ('lang', 'fsdp')), may hold values from -6 to 6
- gate_base: bfloat16 [8192, 16384], P('dp', ('lang', 'fsdp')), may hold values from -0.0625 to 0.0625
- up_base: bfloat16 [8192, 16384], P('dp', ('lang', 'fsdp')), may hold values from -0.0625 to 0.0625
- lang_delta: bfloat16 [4, 2, 4, 4, 32768], P('lang', 'fsdp'), may hold values from -0.1796875 to 0.1796875
- lang_cell: int32 [4, 2, 4, 4], P('lang', 'fsdp'), may hold values from -1 to 1023, as said below
- group_lang: int32 [4], P('dp'), may hold values from 0 to 3
- task_delta: bfloat16 [128, 32768], P(('lang', 'fsdp')), may hold values from -0.1796875 to 0.1796875
- task_slab: int32 [128, 1], P(('lang', 'fsdp')), may hold values from 0 to 1; in each aligned block of 16 rows (0 to 15, 16 to 31, ...) at most 8 rows name the same one
- task_cell: int32 [128, 1], P(('lang', 'fsdp')), may hold values from 0 to 1023
Outputs:
- grad_input: bfloat16 [1024, 8192], P('dp', ('lang', 'fsdp'))
- task_grad: float32 [128, 32768], P(('lang', 'fsdp'))
The draws below stay inside these ranges and needn't reach their ends.
Inputs may be any that keep to these rules, and one draw needn't show every extreme that they name: `lang_cell`: -1 marks an empty slot; every other entry is a cell of the slab. In every draw the list of slab 0 is full for every language. `task_slab`: among the 16 task blocks of one device, no slab is named more than 8 times; some slab is named exactly 8 times.
All inputs are finite; a program needn't handle non-finite values.
Results may differ from the reference program's by a relative error of at most 0.0063.
Values may be sent and summed in bfloat16 or wider, within the bound.
A program may use at most 448 MiB of HBM per device.

```python
import math
import jax
import jax.numpy as jnp
import numpy as np
from jax import lax

D = 8192
FF = 16384
BLK = 128
TG = 256
NLB = 4
NTD = 16
LANGS = 4
FSDP_WAYS = 2
SLAB_BLOCKS = 16
CAP = 8
TOKENS = 1024
TASKS = 128
N_LANG = 4
N_FSDP = 2
N_DP = 4


def draw_lang_cell(key, part):
    key = jax.random.fold_in(key, 11)
    key_cells, key_counts = jax.random.split(key)
    cell_total = D // BLK * (FF // (N_LANG * N_FSDP) // BLK)
    cell_ids = jax.random.randint(key_cells, (N_LANG, N_FSDP, N_LANG, NLB), 0, cell_total)
    how_many = jax.random.randint(key_counts, (N_LANG, N_FSDP, N_LANG, 1), 1, NLB + 1)
    how_many = how_many.at[:, 0, 0, 0].set(NLB)
    slot_index = jnp.arange(NLB, dtype=jnp.int32)[None, None, None, :]
    return jnp.where(slot_index < how_many, cell_ids, -1).astype(jnp.int32)


def with_ends(entries, key, smallest, largest):
    dims = entries.shape
    place = [jax.random.randint(jax.random.fold_in(key, axis), (), 0, dims[axis]) for axis in range(len(dims))]
    entries = entries.at[tuple(place)].set(smallest)
    longest = dims.index(max(dims))
    place[longest] = (place[longest] + 1) % dims[longest]
    return entries.at[tuple(place)].set(largest)


def levels(key, dims, cuts, least, high):
    loudness, own = 1.0, jax.random.fold_in(key, 6)
    for dim, shards_of in cuts:
        draws = jnp.exp(jax.random.uniform(jax.random.fold_in(own, dim), (shards_of,), jnp.float32, least / len(cuts), high / len(cuts)))
        loudness = loudness * jnp.repeat(draws, dims[dim] // shards_of).reshape([-1 if axis == dim else 1 for axis in range(len(dims))])
    return loudness


def shared_out(rng, own, number, rows, amount, top, bound, skew):
    sequence = jax.random.permutation(rng, amount)
    packed, ordinary = load_shares(amount, rows * top, bound, skew, True), load_shares(amount, rows * top, bound, skew, False)
    places = jnp.arange(amount)

    def named(tallies, rotation):
        used = int((tallies > 0).sum())
        fixed = max(1, used // 4)
        shifted = fixed + (places - fixed + rotation * (used - fixed)) % max(1, amount - fixed)
        return jnp.zeros((amount,), jnp.int32).at[sequence[jnp.where(places < fixed, places, shifted)]].set(jnp.asarray(tallies, jnp.int32))

    tallies = jnp.where(number % 4 == 0, named(packed, number // 4), named(ordinary, number - number // 4 - 1))
    mixed = jax.random.permutation(jax.random.fold_in(own, 3), amount)
    source_of, receiver = mixed[0:amount // 2 * 2:2], mixed[1:amount // 2 * 2:2]
    room = jnp.minimum(tallies[source_of] - 1, bound - tallies[receiver]) // 2
    room = jnp.where((source_of == sequence[0]) | (receiver == sequence[0]) | (tallies[receiver] == 0), 0, jnp.maximum(room, 0))
    shifted = jax.random.randint(jax.random.fold_in(own, 4), (amount // 2,), 0, 1 << 20) % (room + 1)
    tallies = tallies.at[source_of].add(-shifted).at[receiver].add(shifted)
    members = jnp.searchsorted(jnp.cumsum(tallies), jnp.arange(rows * top), side="right").astype(jnp.int32)
    table = members.reshape(top, rows).T
    table = table[jax.random.permutation(jax.random.fold_in(own, 1), rows)]
    rotation = jax.random.randint(jax.random.fold_in(own, 2), (rows, 1), 0, top)
    return jnp.take_along_axis(table, (jnp.arange(top)[None, :] + rotation) % top, axis=1)


def load_shares(count, total, bound, slope, full):
    loads = [(1 << 20) // math.isqrt(standing ** slope) + 1 for standing in range(1, count + 1)]
    largest = bound if full else min(bound, max(-(-total // count), total * loads[0] // sum(loads)))
    least = 1 if total - largest >= count - 1 else 0
    counts, spare = [largest] + [least] * (count - 1), total - largest - least * (count - 1)
    while spare > 0:
        candidates = [i for i in range(1, count) if counts[i] < largest] or [i for i in range(1, count) if counts[i] < bound]
        pool, budget = sum([loads[i] for i in candidates]), spare
        for i in candidates:
            extra = min(bound - counts[i], max(1, budget * loads[i] // pool), spare)
            counts[i] = counts[i] + extra
            spare = spare - extra
    return np.array(counts)


def gaussian(stream_key, shape, scale, bound, pieces=(), held_as=jnp.bfloat16):
    loudness = levels(stream_key, shape, pieces, -0.22, 0.18) if pieces else 1.0
    entries = jax.random.normal(stream_key, shape, jnp.float32) * scale * loudness
    return jnp.minimum(jnp.maximum(entries, -bound), bound).astype(held_as)


def setup_inputs(seed: int = 0) -> dict:
    splits = jax.random.split(jax.random.key(seed), 11)
    tokens_in = gaussian(splits[0], (TOKENS, D), 1.0, 6.0, ((0, 4),))
    cotangent = gaussian(splits[1], (TOKENS, FF), 1.0, 6.0, ((0, 4), (1, 8)))
    gate_base = gaussian(splits[2], (D, FF), D ** -0.5, 0.0625, ((0, 4), (1, 8)))
    up_base = gaussian(splits[3], (D, FF), D ** -0.5, 0.0625, ((0, 4), (1, 8)))
    lang_delta = gaussian(splits[4], (LANGS, FSDP_WAYS, LANGS, NLB, 2 * BLK * BLK), 0.03, 0.1796875, ((0, 4), (1, 2)))
    lang_cell = draw_lang_cell(jax.random.fold_in(splits[10], 71), 0)
    group_lang = with_ends(jax.random.randint(splits[6], (N_DP,), 0, LANGS), jax.random.fold_in(splits[6], 1), 0, LANGS - 1).astype(jnp.int32)
    task_delta = gaussian(splits[7], (TASKS, 2 * BLK * BLK), 0.03, 0.1796875, ((0, 8),))
    task_slab_keys = jax.random.split(jax.random.fold_in(splits[8], 1), TASKS // NTD)
    task_slab_turns = jax.random.permutation(jax.random.fold_in(splits[8], 3), TASKS // NTD)
    task_slab = jax.vmap(lambda own, number: shared_out(jax.random.fold_in(splits[8], 2), own, number, NTD, FSDP_WAYS, 1, CAP, 2))(task_slab_keys, task_slab_turns).reshape((TASKS, 1))
    task_cell = with_ends(jax.random.randint(splits[9], (TASKS, 1), 0, D // BLK * SLAB_BLOCKS), jax.random.fold_in(splits[9], 1), 0, (D // BLK * SLAB_BLOCKS) - 1).astype(jnp.int32)
    return dict(tokens_in=tokens_in, cotangent=cotangent, gate_base=gate_base, up_base=up_base, lang_delta=lang_delta, lang_cell=lang_cell, group_lang=group_lang, task_delta=task_delta, task_slab=task_slab, task_cell=task_cell)


def compose_matrix(base_matrix, row_ids, col_ids, tile_vals):
    changes = jnp.zeros((D // BLK, FF // BLK, BLK, BLK), jnp.float32)
    changes = changes.at[row_ids, col_ids].add(tile_vals.reshape(-1, BLK, BLK))
    changes = changes.transpose(0, 2, 1, 3).reshape(D, FF)
    return (base_matrix.astype(jnp.float32) + changes).astype(jnp.bfloat16)


def backward_parts(gate_pre, up_pre, cot_rows):
    sigmoid_g = jax.nn.sigmoid(gate_pre)
    upstream = cot_rows.astype(jnp.float32)
    d_gate = upstream * up_pre * sigmoid_g * (1.0 + gate_pre * (1.0 - sigmoid_g))
    d_up = upstream * gate_pre * sigmoid_g
    return d_gate.astype(jnp.bfloat16), d_up.astype(jnp.bfloat16)


def reference(tokens_in, cotangent, gate_base, up_base, lang_delta, lang_cell, group_lang, task_delta, task_slab, task_cell):
    tile_size = BLK * BLK
    slab_width = FF // (N_LANG * N_FSDP) // BLK
    slab_number = jnp.arange(N_LANG, dtype=jnp.int32)[None, :] * N_FSDP + jnp.arange(N_FSDP, dtype=jnp.int32)[:, None]
    holder = jnp.arange(task_delta.shape[0], dtype=jnp.int32) // NTD
    task_rows = task_cell[:, 0] // slab_width
    task_cols = ((holder // N_FSDP) * N_FSDP + task_slab[:, 0]) * slab_width + task_cell[:, 0] % slab_width
    task_vals = task_delta.astype(jnp.float32)
    grad_parts = []
    task_sum = jnp.zeros(task_delta.shape, jnp.float32)
    for group_id in range(N_DP):
        language = group_lang[group_id]
        cell_ids = lax.dynamic_index_in_dim(lang_cell, language, 0, keepdims=False)
        lang_vals = lax.dynamic_index_in_dim(lang_delta, language, 0, keepdims=False).astype(jnp.float32)
        filled = cell_ids >= 0
        clamped = jnp.where(filled, cell_ids, 0)
        row_ids = (clamped // slab_width).reshape(-1)
        col_ids = (slab_number[:, :, None] * slab_width + clamped % slab_width).reshape(-1)
        lang_vals = jnp.where(filled[..., None], lang_vals, 0.0).reshape(-1, 2 * tile_size)
        all_rows = jnp.concatenate([row_ids, task_rows])
        all_cols = jnp.concatenate([col_ids, task_cols])
        all_vals = jnp.concatenate([lang_vals, task_vals], axis=0)
        gate_matrix = compose_matrix(gate_base, all_rows, all_cols, all_vals[:, :tile_size])
        up_matrix = compose_matrix(up_base, all_rows, all_cols, all_vals[:, tile_size:])
        tokens_group = tokens_in[group_id * TG:(group_id + 1) * TG]
        cot_group = cotangent[group_id * TG:(group_id + 1) * TG]
        gate_pre = jnp.dot(tokens_group, gate_matrix, preferred_element_type=jnp.float32)
        up_pre = jnp.dot(tokens_group, up_matrix, preferred_element_type=jnp.float32)
        d_gate, d_up = backward_parts(gate_pre, up_pre, cot_group)
        input_grad = jnp.dot(d_gate, gate_matrix.T, preferred_element_type=jnp.float32)
        input_grad = input_grad + jnp.dot(d_up, up_matrix.T, preferred_element_type=jnp.float32)
        grad_parts.append(input_grad.astype(jnp.bfloat16))
        x_tiles = tokens_group.reshape(TG, D // BLK, BLK)[:, task_rows, :].astype(jnp.float32)
        g_tiles = d_gate.reshape(TG, FF // BLK, BLK)[:, task_cols, :].astype(jnp.float32)
        u_tiles = d_up.reshape(TG, FF // BLK, BLK)[:, task_cols, :].astype(jnp.float32)
        gate_grad = jnp.einsum('tmi,tmj->mij', x_tiles, g_tiles).reshape(-1, tile_size)
        up_grad = jnp.einsum('tmi,tmj->mij', x_tiles, u_tiles).reshape(-1, tile_size)
        task_sum = task_sum + jnp.concatenate([gate_grad, up_grad], axis=1)
    return jnp.concatenate(grad_parts, axis=0), task_sum
```

```python
import jax
import jax.numpy as jnp
from jax import lax
from jax.sharding import PartitionSpec as P

D = 8192
BLK = 128
F32 = jnp.float32
BF16 = jnp.bfloat16


def on_device(
    tokens_in,
    cotangent,
    gate_base,
    up_base,
    lang_delta,
    lang_cell,
    group_lang,
    task_delta,
    task_slab,
    task_cell,
):
    tile_size = BLK * BLK
    own_rows, slab_cols = gate_base.shape
    slab_width = slab_cols // BLK
    row_blocks = D // BLK
    own_blocks = own_rows // BLK
    group_rows = tokens_in.shape[0]
    lang_ways, fsdp_ways = lax.axis_size("lang"), lax.axis_size("fsdp")
    groups = lax.axis_size("dp")
    plane = lang_ways * fsdp_ways
    part = lax.axis_index("dp")
    place = lax.axis_index("lang") * fsdp_ways + lax.axis_index("fsdp")

    piece = own_rows // plane
    mine = lax.dynamic_index_in_dim(
        tokens_in.reshape(group_rows, groups, plane, piece), place, 2, keepdims=False
    )
    mine = lax.all_to_all(mine, "dp", split_axis=1, concat_axis=0, tiled=True)
    x_all = lax.all_gather(
        mine.reshape(groups * group_rows, piece), ("lang", "fsdp"), axis=1, tiled=True
    )

    held = task_delta.shape[0]
    capacity = max(2, (held + fsdp_ways - 1) // fsdp_ways)
    target = task_slab[:, 0]
    matches = (target[:, None] == jnp.arange(fsdp_ways, dtype=jnp.int32)[None, :]).astype(jnp.int32)
    slot_of = jnp.sum(jnp.cumsum(matches, axis=0) * matches, axis=1) - 1
    taken = (matches.T[:, None, :] == 1) & (
        slot_of[None, None, :] == jnp.arange(capacity, dtype=jnp.int32)[None, :, None]
    )
    source = jnp.argmax(taken, axis=2)
    send_vals = task_delta[source.reshape(-1)].reshape(fsdp_ways, capacity, 2 * tile_size)
    send_cells = jnp.where(jnp.any(taken, axis=2), task_cell[:, 0][source], -1)
    got_vals = lax.all_to_all(send_vals, "fsdp", split_axis=0, concat_axis=0, tiled=True)
    got_cells = lax.all_to_all(send_cells, "fsdp", split_axis=0, concat_axis=0, tiled=True)

    lang_vals = lax.all_to_all(lang_delta[0, 0], "lang", split_axis=0, concat_axis=0, tiled=True)
    lang_cells = lax.all_to_all(lang_cell[0, 0], "lang", split_axis=0, concat_axis=0, tiled=True)
    languages = lax.all_gather(group_lang, "dp", axis=0, tiled=True)
    per_lang = lang_cells.shape[1]

    task_cells = got_cells.reshape(-1)
    tiles = jnp.concatenate(
        [got_vals.reshape(-1, 2 * tile_size), lang_vals.reshape(-1, 2 * tile_size)], axis=0
    )
    gate_tiles = tiles[:, :tile_size].reshape(-1, BLK, BLK)
    up_tiles = tiles[:, tile_size:].reshape(-1, BLK, BLK)
    cells = jnp.concatenate([task_cells, lang_cells.reshape(-1)])
    task_slots = task_cells.shape[0]
    lang_of = jnp.concatenate(
        [
            jnp.full((task_slots,), -1, jnp.int32),
            jnp.repeat(jnp.arange(lang_ways, dtype=jnp.int32), per_lang),
        ]
    )
    counted = (cells >= 0)[:, None] & (
        (lang_of < 0)[:, None] | (lang_of[:, None] == languages[None, :])
    )
    safe = jnp.where(cells >= 0, cells, 0)
    row_of, col_of = safe // slab_width, safe % slab_width

    def frozen(weights):
        partial = jnp.dot(x_all, weights, preferred_element_type=F32).astype(BF16)
        return lax.psum_scatter(partial, "dp", scatter_dimension=0, tiled=True).astype(F32)

    gate_frozen, up_frozen = frozen(gate_base), frozen(up_base)

    x_slots = tokens_in.reshape(group_rows, row_blocks, BLK).transpose(1, 0, 2)[row_of]
    counted_here = lax.dynamic_index_in_dim(counted, part, 1, keepdims=False)
    to_cols = (
        counted_here[:, None]
        & (col_of[:, None] == jnp.arange(slab_width, dtype=jnp.int32)[None, :])
    ).astype(BF16)

    def blocks_part(block_tiles):
        products = jnp.einsum(
            "kti,kij->ktj", x_slots, block_tiles, preferred_element_type=F32
        ).astype(BF16)
        placed = jnp.einsum("kc,ktj->ctj", to_cols, products, preferred_element_type=F32)
        return placed.transpose(1, 0, 2).reshape(group_rows, slab_cols)

    gate_pre = gate_frozen + blocks_part(gate_tiles)
    up_pre = up_frozen + blocks_part(up_tiles)
    sigmoid_g = jax.nn.sigmoid(gate_pre)
    upstream = cotangent.astype(F32)
    d_gate = (upstream * up_pre * sigmoid_g * (1.0 + gate_pre * (1.0 - sigmoid_g))).astype(BF16)
    d_up = (upstream * gate_pre * sigmoid_g).astype(BF16)
    g_all = lax.all_gather(d_gate, "dp", axis=0, tiled=True)
    u_all = lax.all_gather(d_up, "dp", axis=0, tiled=True)

    tokens = groups * group_rows
    g_slots = g_all.reshape(tokens, slab_width, BLK).transpose(1, 0, 2)[col_of]
    u_slots = u_all.reshape(tokens, slab_width, BLK).transpose(1, 0, 2)[col_of]
    own_row = row_of - part * own_blocks
    at_row = own_row[:, None] == jnp.arange(own_blocks, dtype=jnp.int32)[None, :]
    to_rows = (counted[:, :, None] & at_row[:, None, :]).astype(BF16)
    products = jnp.einsum("ktj,kij->kti", g_slots, gate_tiles, preferred_element_type=F32)
    products = products + jnp.einsum("ktj,kij->kti", u_slots, up_tiles, preferred_element_type=F32)
    products = products.astype(BF16).reshape(-1, groups, group_rows, BLK)
    placed = jnp.einsum("kgr,kgti->grti", to_rows, products, preferred_element_type=F32)
    contract = (((1,), (1,)), ((), ()))
    total = lax.dot_general(g_all, gate_base, contract, preferred_element_type=F32)
    total = total + lax.dot_general(u_all, up_base, contract, preferred_element_type=F32)
    total = total + placed.transpose(0, 2, 1, 3).reshape(tokens, own_rows)

    out_cols = own_rows // fsdp_ways
    total = total.reshape(groups, group_rows, fsdp_ways, out_cols).transpose(0, 2, 1, 3)
    summed = lax.psum_scatter(
        total.reshape(plane, group_rows, out_cols),
        ("lang", "fsdp"),
        scatter_dimension=0,
        tiled=True,
    )[0].astype(BF16)
    swap = [(l * groups + p, p * groups + l) for l in range(lang_ways) for p in range(groups)]
    grad_input = lax.ppermute(summed, ("lang", "dp"), swap)

    here = (task_cells >= 0) & jnp.any(at_row[:task_slots], axis=1)
    local_row = jnp.clip(own_row[:task_slots], 0, own_blocks - 1)
    x_tiles = x_all.reshape(tokens, own_blocks, BLK).transpose(1, 0, 2)[local_row]
    gate_grad = jnp.einsum("kti,ktj->kij", x_tiles, g_slots[:task_slots], preferred_element_type=F32)
    up_grad = jnp.einsum("kti,ktj->kij", x_tiles, u_slots[:task_slots], preferred_element_type=F32)
    slot_grads = jnp.stack([gate_grad, up_grad], axis=1)
    slot_grads = jnp.where(here[:, None, None, None], slot_grads, 0.0).astype(BF16)
    slot_grads = slot_grads.reshape(fsdp_ways, capacity, 2 * tile_size)
    slot_grads = lax.psum(slot_grads, "dp")
    returned = lax.all_to_all(slot_grads, "fsdp", split_axis=0, concat_axis=0, tiled=True)
    task_grad = returned[target, slot_of].astype(F32)
    return (grad_input, task_grad)


def solution(mesh):
    return jax.shard_map(
        on_device,
        mesh=mesh,
        in_specs=(
            P("dp", None),
            P("dp", ("lang", "fsdp")),
            P("dp", ("lang", "fsdp")),
            P("dp", ("lang", "fsdp")),
            P("lang", "fsdp", None, None, None),
            P("lang", "fsdp", None, None),
            P("dp"),
            P(("lang", "fsdp"), None),
            P(("lang", "fsdp"), None),
            P(("lang", "fsdp"), None),
        ),
        out_specs=(P("dp", ("lang", "fsdp")), P(("lang", "fsdp"), None)),
        check_vma=False,
    )
```

```python
import jax
import jax.numpy as jnp
from jax import lax
from jax.sharding import PartitionSpec as P

D = 8192
BLK = 128
F32 = jnp.float32
BF16 = jnp.bfloat16


def on_device(
    tokens_in,
    cotangent,
    gate_base,
    up_base,
    lang_delta,
    lang_cell,
    group_lang,
    task_delta,
    task_slab,
    task_cell,
):
    tile_size = BLK * BLK
    own_rows, slab_cols = gate_base.shape
    slab_width = slab_cols // BLK
    row_blocks = D // BLK
    own_blocks = own_rows // BLK
    group_rows = tokens_in.shape[0]
    lang_ways, fsdp_ways = lax.axis_size("lang"), lax.axis_size("fsdp")
    groups = lax.axis_size("dp")
    plane = lang_ways * fsdp_ways
    part = lax.axis_index("dp")
    place = lax.axis_index("lang") * fsdp_ways + lax.axis_index("fsdp")

    piece = own_rows // plane
    mine = lax.dynamic_index_in_dim(
        tokens_in.reshape(group_rows, groups, plane, piece), place, 2, keepdims=False
    )
    mine = lax.all_to_all(mine, "dp", split_axis=1, concat_axis=0, tiled=True)
    x_all = lax.all_gather(
        mine.reshape(groups * group_rows, piece), ("lang", "fsdp"), axis=1, tiled=True
    )

    held = task_delta.shape[0]
    capacity = max(2, (held + fsdp_ways - 1) // fsdp_ways)
    target = task_slab[:, 0]
    matches = (target[:, None] == jnp.arange(fsdp_ways, dtype=jnp.int32)[None, :]).astype(jnp.int32)
    slot_of = jnp.sum(jnp.cumsum(matches, axis=0) * matches, axis=1) - 1
    taken = (matches.T[:, None, :] == 1) & (
        slot_of[None, None, :] == jnp.arange(capacity, dtype=jnp.int32)[None, :, None]
    )
    source = jnp.argmax(taken, axis=2)
    send_vals = task_delta[source.reshape(-1)].reshape(fsdp_ways, capacity, 2 * tile_size)
    send_cells = jnp.where(jnp.any(taken, axis=2), task_cell[:, 0][source], -1)
    got_vals = lax.all_to_all(send_vals, "fsdp", split_axis=0, concat_axis=0, tiled=True)
    got_cells = lax.all_to_all(send_cells, "fsdp", split_axis=0, concat_axis=0, tiled=True)

    lang_vals = lax.all_to_all(lang_delta[0, 0], "lang", split_axis=0, concat_axis=0, tiled=True)
    lang_cells = lax.all_to_all(lang_cell[0, 0], "lang", split_axis=0, concat_axis=0, tiled=True)
    languages = lax.all_gather(group_lang, "dp", axis=0, tiled=True)
    per_lang = lang_cells.shape[1]

    task_cells = got_cells.reshape(-1)
    tiles = jnp.concatenate(
        [got_vals.reshape(-1, 2 * tile_size), lang_vals.reshape(-1, 2 * tile_size)], axis=0
    )
    gate_tiles = tiles[:, :tile_size].reshape(-1, BLK, BLK)
    up_tiles = tiles[:, tile_size:].reshape(-1, BLK, BLK)
    cells = jnp.concatenate([task_cells, lang_cells.reshape(-1)])
    task_slots = task_cells.shape[0]
    lang_of = jnp.concatenate(
        [
            jnp.full((task_slots,), -1, jnp.int32),
            jnp.repeat(jnp.arange(lang_ways, dtype=jnp.int32), per_lang),
        ]
    )
    counted = (cells >= 0)[:, None] & (
        (lang_of < 0)[:, None] | (lang_of[:, None] == languages[None, :])
    )
    safe = jnp.where(cells >= 0, cells, 0)
    row_of, col_of = safe // slab_width, safe % slab_width

    half = slab_cols // 2

    def frozen(part_index):
        cols = slice(part_index * half, (part_index + 1) * half)
        partial = jnp.concatenate(
            [
                jnp.dot(x_all, gate_base[:, cols], preferred_element_type=F32).astype(BF16),
                jnp.dot(x_all, up_base[:, cols], preferred_element_type=F32).astype(BF16),
            ],
            axis=1,
        )
        return lax.psum_scatter(partial, "dp", scatter_dimension=0, tiled=True)

    first, second = frozen(0), frozen(1)

    x_slots = tokens_in.reshape(group_rows, row_blocks, BLK).transpose(1, 0, 2)[row_of]
    counted_here = lax.dynamic_index_in_dim(counted, part, 1, keepdims=False)
    to_cols = (
        counted_here[:, None]
        & (col_of[:, None] == jnp.arange(slab_width, dtype=jnp.int32)[None, :])
    ).astype(BF16)

    def blocks_part(block_tiles):
        products = jnp.einsum(
            "kti,kij->ktj", x_slots, block_tiles, preferred_element_type=F32
        ).astype(BF16)
        placed = jnp.einsum("kc,ktj->ctj", to_cols, products, preferred_element_type=F32)
        return placed.transpose(1, 0, 2).reshape(group_rows, slab_cols)

    gate_blocks, up_blocks = blocks_part(gate_tiles), blocks_part(up_tiles)

    def gradients(sums, part_index):
        cols = slice(part_index * half, (part_index + 1) * half)
        gate_pre = sums[:, :half].astype(F32) + gate_blocks[:, cols]
        up_pre = sums[:, half:].astype(F32) + up_blocks[:, cols]
        sigmoid_g = jax.nn.sigmoid(gate_pre)
        upstream = cotangent[:, cols].astype(F32)
        d_gate = upstream * up_pre * sigmoid_g * (1.0 + gate_pre * (1.0 - sigmoid_g))
        d_up = upstream * gate_pre * sigmoid_g
        return jnp.concatenate([d_gate.astype(BF16), d_up.astype(BF16)], axis=1)

    d_first = gradients(first, 0)
    to_right = [(g, g + 1) for g in range(groups - 1)]
    to_left = [(g + 1, g) for g in range(groups - 1)]
    from_left, from_right = [d_first], [d_first]
    for _ in range(groups - 1):
        from_left.append(lax.ppermute(from_left[-1], "dp", to_right))
        from_right.append(lax.ppermute(from_right[-1], "dp", to_left))
    ordered = []
    for g in range(groups):
        value = d_first
        for distance in range(1, groups):
            value = jnp.where(part - g == distance, from_left[distance], value)
            value = jnp.where(g - part == distance, from_right[distance], value)
        ordered.append(value)
    all_first = jnp.concatenate(ordered, axis=0)
    contract = (((1,), (1,)), ((), ()))

    def frozen_back(d_all, part_index):
        cols = slice(part_index * half, (part_index + 1) * half)
        gate_term = lax.dot_general(
            d_all[:, :half], gate_base[:, cols], contract, preferred_element_type=F32
        )
        return gate_term + lax.dot_general(
            d_all[:, half:], up_base[:, cols], contract, preferred_element_type=F32
        )

    all_first, second = lax.optimization_barrier((all_first, second))
    all_second = lax.all_gather(gradients(second, 1), "dp", axis=0, tiled=True)
    total_first = frozen_back(all_first, 0)
    total_first, all_second = lax.optimization_barrier((total_first, all_second))
    g_all = jnp.concatenate([all_first[:, :half], all_second[:, :half]], axis=1)
    u_all = jnp.concatenate([all_first[:, half:], all_second[:, half:]], axis=1)

    tokens = groups * group_rows
    g_slots = g_all.reshape(tokens, slab_width, BLK).transpose(1, 0, 2)[col_of]
    u_slots = u_all.reshape(tokens, slab_width, BLK).transpose(1, 0, 2)[col_of]
    own_row = row_of - part * own_blocks
    at_row = own_row[:, None] == jnp.arange(own_blocks, dtype=jnp.int32)[None, :]
    to_rows = (counted[:, :, None] & at_row[:, None, :]).astype(BF16)
    products = jnp.einsum("ktj,kij->kti", g_slots, gate_tiles, preferred_element_type=F32)
    products = products + jnp.einsum("ktj,kij->kti", u_slots, up_tiles, preferred_element_type=F32)
    products = products.astype(BF16).reshape(-1, groups, group_rows, BLK)
    placed = jnp.einsum("kgr,kgti->grti", to_rows, products, preferred_element_type=F32)
    total = total_first + frozen_back(all_second, 1)
    total = (total + placed.transpose(0, 2, 1, 3).reshape(tokens, own_rows)).astype(BF16)

    out_cols = own_rows // fsdp_ways
    total = total.reshape(groups, group_rows, fsdp_ways, out_cols).transpose(0, 2, 1, 3)
    terms = lax.all_to_all(
        total.reshape(plane, group_rows, out_cols),
        ("lang", "fsdp"),
        split_axis=0,
        concat_axis=0,
        tiled=True,
    )
    summed = jnp.sum(terms.astype(F32), axis=0).astype(BF16)
    swap = [(l * groups + p, p * groups + l) for l in range(lang_ways) for p in range(groups)]
    grad_input = lax.ppermute(summed, ("lang", "dp"), swap)

    here = (task_cells >= 0) & jnp.any(at_row[:task_slots], axis=1)
    local_row = jnp.clip(own_row[:task_slots], 0, own_blocks - 1)
    x_tiles = x_all.reshape(tokens, own_blocks, BLK).transpose(1, 0, 2)[local_row]
    gate_grad = jnp.einsum("kti,ktj->kij", x_tiles, g_slots[:task_slots], preferred_element_type=F32)
    up_grad = jnp.einsum("kti,ktj->kij", x_tiles, u_slots[:task_slots], preferred_element_type=F32)
    slot_grads = jnp.stack([gate_grad, up_grad], axis=1)
    slot_grads = jnp.where(here[:, None, None, None], slot_grads, 0.0).astype(BF16)
    slot_grads = slot_grads.reshape(fsdp_ways, capacity, 2 * tile_size)
    slot_grads = lax.psum(slot_grads, "dp")
    returned = lax.all_to_all(slot_grads, "fsdp", split_axis=0, concat_axis=0, tiled=True)
    task_grad = returned[target, slot_of].astype(F32)
    return (grad_input, task_grad)


def solution(mesh):
    return jax.shard_map(
        on_device,
        mesh=mesh,
        in_specs=(
            P("dp", None),
            P("dp", ("lang", "fsdp")),
            P("dp", ("lang", "fsdp")),
            P("dp", ("lang", "fsdp")),
            P("lang", "fsdp", None, None, None),
            P("lang", "fsdp", None, None),
            P("dp"),
            P(("lang", "fsdp"), None),
            P(("lang", "fsdp"), None),
            P(("lang", "fsdp"), None),
        ),
        out_specs=(P("dp", ("lang", "fsdp")), P(("lang", "fsdp"), None)),
        check_vma=False,
    )
```
